32 devices in a mesh: seq: 4 (over y, core), leaf: 8 (over z, x).
Axes of the slice: x: 2, y: 2, z: 4, core: 2. Of those that a mesh axis runs over, the one named last changes fastest.
Arguments:
- queries: bfloat16 [64, 4, 4096], P('leaf'), may hold values from -32 to 32
- prompt_kv: bfloat16 [2, 5120, 512], P(None, 'seq'), may hold values from -8 to 8
- node_kv: bfloat16 [2, 128, 256, 512], P(None, 'leaf', 'seq'), may hold values from -8 to 8
- node_lengths: int32 [128], P('leaf'), may hold values from 128 to 256, as said below
- ancestors: int32 [64, 10], P('leaf'), may hold values from -1 to 127, as said below
Outputs:
- attended: bfloat16 [64, 4, 4096], P('leaf', None, 'seq')
The draws below stay inside these ranges and needn't reach their ends.
Inputs may be any that keep to these rules, and one draw needn't show every extreme that they name: `ancestors`: each entry is -1 or a node id, owner * 16 + slot, whose owner is an index of leaf. The last entry of every row is the leaf's own node, owned by the index of leaf that holds the leaf. A node whose owner is not the index of leaf holding the leaf sits in slot 15 of its owner, and each owner holds one such node at most. `node_lengths`: multiples of 128.
All inputs are finite; a program needn't handle non-finite values.
Results may differ from the reference program's by a relative error of at most 0.0028.
Values may be sent and summed in bfloat16 or wider, within the bound.
A program may use at most 64 MiB of HBM per device.

```python
import math
import jax
import jax.numpy as jnp
from jax import lax

HEADS = 16
KV_HEADS = 2
HEAD_DIM = 256
STEPS = 4
DEPTH = 10
BLOCK = 128
NODE_LEN = 256
LEAF_DEV = 8
P_DEV = 1280
LEAVES = 64
PROMPT = 5120
NODE_DEV = 16
NODES = 128
TOK_SEQ = 64
N_SEQ = 4


def draw_queries(key, part):
    key = jax.random.fold_in(key, 1)
    entries = jnp.clip(1.25 * jax.random.normal(key, (LEAVES, STEPS, HEADS * HEAD_DIM), jnp.float32), -6.0, 6.0)
    return entries.astype(jnp.bfloat16)


def draw_prompt_kv(key, part):
    key = jax.random.fold_in(key, 2)
    entries = jnp.clip(2.0 * jax.random.normal(key, (2, PROMPT, KV_HEADS * HEAD_DIM), jnp.float32), -8.0, 8.0)
    return entries.astype(jnp.bfloat16)


def draw_node_lengths(key, part):
    key = jax.random.fold_in(key, 3)
    block_counts = jax.random.randint(key, (NODES,), 1, NODE_LEN // BLOCK + 1)
    block_counts = block_counts.at[0].set(NODE_LEN // BLOCK).at[1].set(1)
    return (BLOCK * block_counts).astype(jnp.int32)


def draw_ancestors(key, part):
    key = jax.random.fold_in(key, 4)
    dev_count = LEAVES // LEAF_DEV
    lower_levels = LEAF_DEV.bit_length()
    upper_levels = DEPTH - lower_levels
    placed = jax.random.permutation(jax.random.fold_in(key, 1), dev_count).astype(jnp.int32)
    holder = jnp.zeros((dev_count,), jnp.int32).at[placed].set(jnp.arange(dev_count, dtype=jnp.int32))
    leaf_ids = jnp.arange(LEAVES, dtype=jnp.int32)
    device_ids = leaf_ids // LEAF_DEV
    local_ids = leaf_ids % LEAF_DEV
    position = placed[device_ids]
    bounds = jax.random.randint(jax.random.fold_in(key, 2), (dev_count,), 0, lower_levels)
    extra_depth = jax.random.randint(jax.random.fold_in(key, 3), (LEAVES,), 0, bounds[device_ids] + 1)
    extra_depth = jnp.where(local_ids == 0, lower_levels - 1, extra_depth)
    columns = []
    for level in range(DEPTH):
        if level < upper_levels:
            span_size = 2 ** (upper_levels - level)
            if span_size > dev_count:
                columns.append(jnp.full((LEAVES,), -1, jnp.int32))
            else:
                middle = position // span_size * span_size + span_size // 2
                columns.append(holder[middle] * NODE_DEV + NODE_DEV - 1)
        else:
            depth_local = level - upper_levels
            group_leaves = LEAF_DEV >> depth_local
            node_ids = device_ids * NODE_DEV + (2 ** depth_local - 1) + local_ids // group_leaves
            if depth_local < lower_levels - 1:
                node_ids = jnp.where(depth_local < extra_depth, node_ids, -1)
            columns.append(node_ids)
    return jnp.stack(columns, axis=1).astype(jnp.int32)


def shard_levels(rng, extent, pieces, smallest, high):
    gain, own = 1.0, jax.random.fold_in(rng, 6)
    for dim, shards_of in pieces:
        draws = jnp.exp(jax.random.uniform(jax.random.fold_in(own, dim), (shards_of,), jnp.float32, smallest / len(pieces), high / len(pieces)))
        gain = gain * jnp.repeat(draws, extent[dim] // shards_of).reshape([-1 if axis == dim else 1 for axis in range(len(extent))])
    return gain


def normal_values(own_key, shape, deviation, reach, shards=(), kind=jnp.bfloat16):
    array = jax.random.normal(own_key, shape, jnp.float32) * deviation
    if len(shards) > 0:
        array = shard_levels(own_key, shape, shards, -0.22, 0.18) * array
    return jnp.clip(array, min=-reach, max=reach).astype(kind)


def setup_inputs(seed: int = 0) -> dict:
    streams_of = jax.random.split(jax.random.key(seed), 6)
    return {
        "queries": draw_queries(jax.random.fold_in(streams_of[5], 71), 0),
        "prompt_kv": draw_prompt_kv(jax.random.fold_in(streams_of[5], 71), 0),
        "node_kv": normal_values(streams_of[2], (2, NODES, NODE_LEN, KV_HEADS * HEAD_DIM), 2.0, 8.0, ((1, 8), (2, 4))),
        "node_lengths": draw_node_lengths(jax.random.fold_in(streams_of[5], 71), 0),
        "ancestors": draw_ancestors(jax.random.fold_in(streams_of[5], 71), 0),
    }


def combine_parts(first_part, second_part):
    first_max, first_total, first_sum = first_part
    second_max, second_total, second_sum = second_part
    top_max = jnp.maximum(first_max, second_max)
    first_weight = jnp.exp(first_max - top_max)
    second_weight = jnp.exp(second_max - top_max)
    return (top_max, first_total * first_weight + second_total * second_weight, first_sum * first_weight[..., None] + second_sum * second_weight[..., None])

def block_parts(block_id, query_rows, prompt_kv, node_kv, node_lengths, ancestors):
    leaf_count, step_count = (query_rows.shape[0], query_rows.shape[1])
    score_scale = 1.0 / math.sqrt(HEAD_DIM)
    prompt_block = lax.dynamic_slice_in_dim(prompt_kv, (block_id * P_DEV).astype(jnp.int32), P_DEV, 1).astype(jnp.float32)
    prompt_keys = prompt_block[0].reshape(P_DEV, KV_HEADS, HEAD_DIM)
    prompt_values = prompt_block[1].reshape(P_DEV, KV_HEADS, HEAD_DIM)
    prompt_scores = jnp.einsum('lskgd,pkd->lskgp', query_rows, prompt_keys) * score_scale
    node_block = lax.dynamic_slice_in_dim(node_kv, (block_id * TOK_SEQ).astype(jnp.int32), TOK_SEQ, 2)
    safe_ids = jnp.maximum(ancestors, 0)
    picked = node_block[:, safe_ids].astype(jnp.float32)
    lengths = node_lengths[safe_ids]
    position = block_id * TOK_SEQ + jnp.arange(TOK_SEQ, dtype=jnp.int32)
    present = (ancestors >= 0)[:, :, None] & (position[None, None, :] < lengths[:, :, None])
    step_ids = jnp.arange(step_count, dtype=jnp.int32)
    own_limit = lengths[:, -1][:, None] - step_count + step_ids[None, :]
    last_level = jnp.arange(DEPTH, dtype=jnp.int32) == DEPTH - 1
    causal = jnp.logical_not(last_level)[None, None, :, None] | (position[None, None, None, :] <= own_limit[:, :, None, None])
    allowed = present[:, None] & causal
    node_keys = picked[0].reshape(leaf_count, DEPTH, TOK_SEQ, KV_HEADS, HEAD_DIM)
    node_values = picked[1].reshape(leaf_count, DEPTH, TOK_SEQ, KV_HEADS, HEAD_DIM)
    node_scores = jnp.einsum('lskgd,ljtkd->lskgjt', query_rows, node_keys) * score_scale
    node_scores = jnp.where(allowed[:, :, None, None], node_scores, -jnp.inf)
    block_max = jnp.maximum(lax.optimization_barrier(jnp.max(prompt_scores, axis=-1)), lax.optimization_barrier(jnp.max(node_scores, axis=(-2, -1))))
    prompt_weights = jnp.exp(prompt_scores - block_max[..., None])
    node_weights = jnp.exp(node_scores - block_max[..., None, None])
    block_total = lax.optimization_barrier(jnp.sum(prompt_weights, axis=-1)) + lax.optimization_barrier(jnp.sum(node_weights, axis=(-2, -1)))
    prompt_rounded = lax.optimization_barrier(prompt_weights.astype(jnp.bfloat16)).astype(jnp.float32)
    node_rounded = lax.optimization_barrier(node_weights.astype(jnp.bfloat16)).astype(jnp.float32)
    block_sum = jnp.einsum('lskgp,pkd->lskgd', prompt_rounded, prompt_values)
    block_sum = block_sum + jnp.einsum('lskgjt,ljtkd->lskgd', node_rounded, node_values)
    return (block_max, block_total, block_sum)

def reference(queries, prompt_kv, node_kv, node_lengths, ancestors):
    leaf_count, step_count, feat_width = queries.shape
    group_size = HEADS // KV_HEADS
    query_rows = queries.astype(jnp.float32).reshape(leaf_count, step_count, KV_HEADS, group_size, HEAD_DIM)

    def visit_block(carry, block_id):
        block_part = block_parts(block_id, query_rows, prompt_kv, node_kv, node_lengths, ancestors)
        return (combine_parts(carry, block_part), None)
    row_shape = (leaf_count, step_count, KV_HEADS, group_size)
    start_carry = (jnp.full(row_shape, -jnp.inf, jnp.float32), jnp.zeros(row_shape, jnp.float32), jnp.zeros(row_shape + (HEAD_DIM,), jnp.float32))
    final_carry, _ = lax.scan(visit_block, start_carry, jnp.arange(N_SEQ, dtype=jnp.int32))
    denominator = final_carry[1]
    numerator = final_carry[2]
    return (numerator / denominator[..., None]).reshape(leaf_count, step_count, feat_width).astype(jnp.bfloat16)
```

```python
import functools
import math

import jax
import jax.numpy as jnp
from jax import lax
from jax.experimental import pallas as pl
from jax.experimental.pallas import tpu as pltpu
from jax.sharding import PartitionSpec as P

HEADS = 16
KV_HEADS = 2
HEAD_DIM = 256
GROUP = HEADS // KV_HEADS
HIDDEN = -1e30
LOG2E = 1.4426950408889634
MESH = pl.DeviceIdType.MESH


def scores_of(q, keys):
    dims = (((1,), (1,)), ((), ()))
    raw = lax.dot_general(q, keys, dims, preferred_element_type=jnp.float32)
    return raw * (LOG2E / math.sqrt(HEAD_DIM))


def biased(scores, bias):
    rows, cols = scores.shape
    per = bias.shape[0]
    return (scores.reshape(rows // per, per, cols) + bias[None]).reshape(rows, cols)


def bias_of(count):
    extra = jnp.where(count > 1.5, jnp.log(jnp.maximum(count, 1.0)) * LOG2E, 0.0)
    return jnp.where(count > 0.5, extra, HIDDEN)


def mix(p, values):
    return jnp.dot(p.astype(jnp.bfloat16), values, preferred_element_type=jnp.float32)


def merge(one, two):
    m1, l1, a1 = one
    m2, l2, a2 = two
    top = jnp.maximum(m1, m2)
    w1, w2 = jnp.exp2(m1 - top), jnp.exp2(m2 - top)
    return top, l1 * w1 + l2 * w2, a1 * w1 + a2 * w2


def packed(m, l):
    lane = lax.broadcasted_iota(jnp.int32, (m.shape[0], 128), 1)
    return jnp.where(lane == 0, m, jnp.where(lane == 1, l, 0.0))


def kernel(
    seq_size, leaf_size, steps,
    q_hbm, prompt_hbm, node_hbm, len_ref, anc_ref, out_ref,
    q_in, prompt, node, qs, shared, lens, bias_ref,
    acc, stat, stat_t, got_acc, got_stat, pair_out, pair_in,
    load_sem, slot_send, slot_recv, len_send, len_recv,
    block_send, block_recv, acc_send, acc_recv, stat_send, stat_recv, pair_sem,
):
    pairs = seq_size // 2
    per_kv = pairs // KV_HEADS
    pair_rows = (HEADS // pairs) * q_in.shape[0]
    half_rows = pair_rows // 2
    rows = q_in.shape[0]
    slots, tokens = node.shape[1], node.shape[2]
    levels = anc_ref.shape[1]
    far = leaf_size // 2
    seq, leaf = lax.axis_index("seq"), lax.axis_index("leaf")
    pair, core = seq // 2, lax.rem(seq, 2)
    kv = pair // per_kv
    place = lax.rem(pair, per_kv)
    line, side = leaf // 2, lax.rem(leaf, 2)
    sibling = (pair * 2 + 1 - core, leaf)
    across = (seq, line * 2 + 1 - side)

    def pair_at(p):
        return (p * 2 + core, leaf)

    def leaf_at(n):
        return (seq, n)

    def kv_cols(k):
        return pl.ds(pl.multiple_of(k * HEAD_DIM, HEAD_DIM), HEAD_DIM)

    loads = [
        pltpu.make_async_copy(q_hbm, q_in, load_sem.at[0]),
        pltpu.make_async_copy(node_hbm, node, load_sem.at[1]),
        pltpu.make_async_copy(prompt_hbm, prompt, load_sem.at[2]),
    ]
    for load in loads:
        load.start()

    barrier = pltpu.get_barrier_semaphore()
    for d in range(1, pairs):
        pl.semaphore_signal(barrier, inc=1, device_id=pair_at(lax.rem(pair + d, pairs)), device_id_type=MESH)
    for d in range(1, leaf_size):
        pl.semaphore_signal(barrier, inc=1, device_id=leaf_at(lax.rem(leaf + d, leaf_size)), device_id_type=MESH)
    pl.semaphore_signal(barrier, inc=1, device_id=sibling, device_id_type=MESH)
    lens[pl.ds(leaf, 1)] = jnp.full((1, 8, 128), len_ref[slots - 1], jnp.int32)
    pl.semaphore_wait(barrier, pairs + leaf_size - 1)

    slot_copies = []
    for d in range(1, pairs):
        to = lax.rem(pair + d, pairs)
        slot_copies.append(pltpu.make_async_remote_copy(
            src_ref=node_hbm.at[:, slots - 1, :, kv_cols(to // per_kv)],
            dst_ref=shared.at[leaf, :, pair],
            send_sem=slot_send.at[d], recv_sem=slot_recv.at[d],
            device_id=pair_at(to), device_id_type=MESH,
        ))
        slot_copies[-1].start()
    own_slot = pltpu.make_async_copy(
        node_hbm.at[:, slots - 1, :, kv_cols(kv)], shared.at[leaf, :, pair], load_sem.at[3]
    )
    own_slot.start()
    len_copies = []
    for d in range(1, leaf_size):
        len_copies.append(pltpu.make_async_remote_copy(
            src_ref=lens.at[leaf], dst_ref=lens.at[leaf],
            send_sem=len_send.at[d], recv_sem=len_recv.at[d],
            device_id=leaf_at(lax.rem(leaf + d, leaf_size)), device_id_type=MESH,
        ))
        len_copies[-1].start()

    loads[0].wait()
    for h in range(HEADS):
        qs[h // GROUP, (h % GROUP) * rows:(h % GROUP + 1) * rows, :] = q_in[:, h * HEAD_DIM:(h + 1) * HEAD_DIM]

    for copy in slot_copies:
        copy.wait_recv()
    own_slot.wait()

    def block_copy(source, target, n):
        return pltpu.make_async_remote_copy(
            src_ref=shared.at[source], dst_ref=shared.at[source],
            send_sem=block_send.at[n], recv_sem=block_recv.at[n],
            device_id=target, device_id_type=MESH,
        )

    own_across = block_copy(leaf, across, 0)
    own_across.start()
    along = []
    for d in range(1, far):
        along.append(block_copy(leaf, leaf_at(lax.rem(line + d, far) * 2 + side), d))
        along[-1].start()

    anc = jnp.zeros((rows, levels), jnp.int32)
    row_leaf = lax.broadcasted_iota(jnp.int32, (rows, levels), 0) // steps
    for n in range(rows // steps):
        anc = jnp.where(row_leaf == n, anc_ref[n:n + 1, :], anc)
    width = slots * tokens
    col = lax.broadcasted_iota(jnp.int32, (1, width), 1)
    col_slot = col // tokens
    position = seq * tokens + col - col_slot * tokens
    held = jnp.zeros((1, width), jnp.int32)
    for n in range(slots):
        held = jnp.where(col_slot == n, len_ref[n], held)
    ident = leaf * slots + col_slot
    inside = position < held
    count = jnp.zeros((rows, width), jnp.float32)
    for level in range(levels - 1):
        count += jnp.where(anc[:, level:level + 1] == ident, 1.0, 0.0)
    step = lax.rem(lax.broadcasted_iota(jnp.int32, (rows, width), 0), steps)
    last = (anc[:, levels - 1:] == ident) & (position <= held - steps + step)
    count += jnp.where(last, 1.0, 0.0)
    bias_ref[...] = bias_of(jnp.where(inside, count, 0.0))

    loads[1].wait()
    loads[2].wait()

    def main(k, n):
        q = qs[k]
        cols = kv_cols(k)
        first = scores_of(q, prompt[0, :, cols])
        second = biased(scores_of(q, node[0, :, :, cols].reshape(width, HEAD_DIM)), bias_ref[...])
        m = jnp.maximum(jnp.max(first, axis=1, keepdims=True), jnp.max(second, axis=1, keepdims=True))
        first = jnp.exp2(first - m)
        second = jnp.exp2(second - m)
        l = jnp.sum(first, axis=1, keepdims=True) + jnp.sum(second, axis=1, keepdims=True)
        acc[n] = mix(first, prompt[1, :, cols]) + mix(second, node[1, :, :, cols].reshape(width, HEAD_DIM))
        both = packed(m, l)
        stat[n] = both
        stat_t[n] = both.T[:8]

    def send_part(n, place_there, to, slot):
        part = pl.ds(pl.multiple_of(place_there * pair_rows, pair_rows), pair_rows)
        copies = [
            pltpu.make_async_remote_copy(
                src_ref=acc.at[n, part], dst_ref=got_acc.at[slot],
                send_sem=acc_send.at[slot], recv_sem=acc_recv.at[slot],
                device_id=pair_at(to), device_id_type=MESH,
            ),
            pltpu.make_async_remote_copy(
                src_ref=stat_t.at[n], dst_ref=got_stat.at[slot],
                send_sem=stat_send.at[slot], recv_sem=stat_recv.at[slot],
                device_id=pair_at(to), device_id_type=MESH,
            ),
        ]
        for copy in copies:
            copy.start()
        return copies

    forwards = []

    def forward(d):
        along[d - 1].wait_recv()
        source = lax.rem(line + far - d, far) * 2 + side
        forwards.append(block_copy(source, across, far + d - 1))
        forwards[-1].start()

    main(1 - kv, 0)
    parts = []
    for n in range(per_kv):
        place_there = lax.rem(place + n, per_kv)
        parts += send_part(0, place_there, (1 - kv) * per_kv + place_there, n)
    forward(1)
    main(kv, 1)
    for n in range(1, per_kv):
        place_there = lax.rem(place + n, per_kv)
        parts += send_part(1, place_there, kv * per_kv + place_there, per_kv + n - 1)

    mine = pl.ds(pl.multiple_of(place * pair_rows, pair_rows), pair_rows)
    q_mine = qs[kv, mine]
    state = (stat[1, mine, 0:1], stat[1, mine, 1:2], acc[1, mine])

    for copy in len_copies:
        copy.wait_recv()
    span = pairs * tokens
    span_col = lax.broadcasted_iota(jnp.int32, (1, span), 1)
    span_block = span_col // tokens
    span_position = (span_block * 2 + core) * tokens + span_col - span_block * tokens

    def visit(state, source):
        m, l, total = state
        target = source * slots + slots - 1
        count = jnp.zeros((rows, 1), jnp.float32)
        for level in range(levels - 1):
            count += jnp.where(anc[:, level:level + 1] == target, 1.0, 0.0)
        bias = bias_of(jnp.where(span_position < lens[source][0:1, :span], count, 0.0))
        s = biased(scores_of(q_mine, shared[source, 0].reshape(span, HEAD_DIM)), bias)
        top = jnp.maximum(m, jnp.max(s, axis=1, keepdims=True))
        p = jnp.exp2(s - top)
        w = jnp.exp2(m - top)
        return (
            top,
            l * w + jnp.sum(p, axis=1, keepdims=True),
            total * w + mix(p, shared[source, 1].reshape(span, HEAD_DIM)),
        )

    def line_source(d, s):
        return lax.rem(line + far - d, far) * 2 + s

    for d in range(2, far):
        forward(d)
        if d == 2:
            own_across.wait_recv()
            state = visit(state, line_source(0, 1 - side))
        state = visit(state, line_source(d - 1, side))
    state = visit(state, line_source(far - 1, side))

    for n in range(pairs - 1):
        parts[2 * n].wait_recv()
        parts[2 * n + 1].wait_recv()
        stats = jnp.concatenate([got_stat[n], jnp.zeros((120, GROUP * rows), jnp.float32)], axis=0).T
        stat[0] = stats
        state = merge(state, (stat[0, mine, 0:1], stat[0, mine, 1:2], got_acc[n]))

    for d in range(1, far):
        forwards[d - 1].wait_recv()
        state = visit(state, line_source(d, 1 - side))

    pair_out[:, HEAD_DIM:] = packed(state[0], state[1])
    pair_out[:, :HEAD_DIM] = state[2]

    def half(n):
        return pl.ds(pl.multiple_of(n * half_rows, half_rows), half_rows)

    swap = pltpu.make_async_remote_copy(
        src_ref=pair_out.at[half(1 - core)], dst_ref=pair_in,
        send_sem=pair_sem.at[0], recv_sem=pair_sem.at[1],
        device_id=sibling, device_id_type=MESH,
    )
    swap.start()
    kept = pair_out[half(core)]
    swap.wait_recv()
    came = pair_in[...]
    _, l, total = merge(
        (kept[:, HEAD_DIM:HEAD_DIM + 1], kept[:, HEAD_DIM + 1:HEAD_DIM + 2], kept[:, :HEAD_DIM]),
        (came[:, HEAD_DIM:HEAD_DIM + 1], came[:, HEAD_DIM + 1:HEAD_DIM + 2], came[:, :HEAD_DIM]),
    )
    result = (total / l).astype(out_ref.dtype)
    for h in range(half_rows // rows):
        out_ref[:, h * HEAD_DIM:(h + 1) * HEAD_DIM] = result[h * rows:(h + 1) * rows]

    for copy in slot_copies + len_copies + [own_across] + along + forwards + parts + [swap]:
        copy.wait_send()


def shards(seq_size, leaf_size, queries, prompt_kv, node_kv, node_lengths, ancestors):
    leaves, steps, feats = queries.shape
    rows = leaves * steps
    slots, tokens, wide = node_kv.shape[1:]
    pairs = seq_size // 2
    pair_rows = (HEADS // pairs) * rows
    span = pairs * tokens
    kv_rows = GROUP * rows
    dma = pltpu.SemaphoreType.DMA
    out = pl.pallas_call(
        functools.partial(kernel, seq_size, leaf_size, steps),
        out_shape=jax.ShapeDtypeStruct((rows, feats // seq_size), jnp.bfloat16),
        in_specs=[pl.BlockSpec(memory_space=pl.ANY)] * 3
        + [pl.BlockSpec(memory_space=pltpu.SMEM), pl.BlockSpec(memory_space=pltpu.VMEM)],
        out_specs=pl.BlockSpec(memory_space=pltpu.VMEM),
        scratch_shapes=[
            pltpu.VMEM((rows, feats), jnp.bfloat16),
            pltpu.VMEM(prompt_kv.shape, jnp.bfloat16),
            pltpu.VMEM(node_kv.shape, jnp.bfloat16),
            pltpu.VMEM((KV_HEADS, kv_rows, HEAD_DIM), jnp.bfloat16),
            pltpu.VMEM((leaf_size, 2, pairs, tokens, HEAD_DIM), jnp.bfloat16),
            pltpu.VMEM((leaf_size, 8, 128), jnp.int32),
            pltpu.VMEM((rows, slots * tokens), jnp.float32),
            pltpu.VMEM((2, kv_rows, HEAD_DIM), jnp.float32),
            pltpu.VMEM((2, kv_rows, 128), jnp.float32),
            pltpu.VMEM((2, 8, kv_rows), jnp.float32),
            pltpu.VMEM((pairs - 1, pair_rows, HEAD_DIM), jnp.float32),
            pltpu.VMEM((pairs - 1, 8, kv_rows), jnp.float32),
            pltpu.VMEM((pair_rows, HEAD_DIM + 128), jnp.float32),
            pltpu.VMEM((pair_rows // 2, HEAD_DIM + 128), jnp.float32),
            dma((4,)),
            dma((pairs,)), dma((pairs,)),
            dma((leaf_size,)), dma((leaf_size,)),
            dma((leaf_size,)), dma((leaf_size,)),
            dma((pairs,)), dma((pairs,)),
            dma((pairs,)), dma((pairs,)),
            dma((2,)),
        ],
        compiler_params=pltpu.CompilerParams(
            collective_id=0, has_side_effects=True, vmem_limit_bytes=48 * 1024 * 1024
        ),
    )(queries.reshape(rows, feats), prompt_kv, node_kv, node_lengths, ancestors)
    return out.reshape(leaves, steps, feats // seq_size)


def solution(mesh):
    placed = (
        P("leaf", None, None),
        P(None, "seq", None),
        P(None, "leaf", "seq", None),
        P("leaf"),
        P("leaf", None),
    )
    return jax.shard_map(
        functools.partial(shards, mesh.shape["seq"], mesh.shape["leaf"]),
        mesh=mesh, in_specs=placed, out_specs=P("leaf", None, "seq"), check_vma=False,
    )
```

```python
import functools
import math

import jax
import jax.numpy as jnp
from jax import lax
from jax.experimental import pallas as pl
from jax.experimental.pallas import tpu as pltpu
from jax.sharding import PartitionSpec as P

HEADS = 16
KV_HEADS = 2
HEAD_DIM = 256
GROUP = HEADS // KV_HEADS
HIDDEN = -1e30
LOG2E = 1.4426950408889634
MESH = pl.DeviceIdType.MESH


def scores_of(q, keys):
    dims = (((1,), (1,)), ((), ()))
    raw = lax.dot_general(q, keys, dims, preferred_element_type=jnp.float32)
    return raw * (LOG2E / math.sqrt(HEAD_DIM))


def biased(scores, bias):
    rows, cols = scores.shape
    per = bias.shape[0]
    return (scores.reshape(rows // per, per, cols) + bias[None]).reshape(rows, cols)


def bias_of(count):
    extra = jnp.where(count > 1.5, jnp.log(jnp.maximum(count, 1.0)) * LOG2E, 0.0)
    return jnp.where(count > 0.5, extra, HIDDEN)


def mix(p, values):
    return jnp.dot(p.astype(jnp.bfloat16), values, preferred_element_type=jnp.float32)


def merge(one, two):
    m1, l1, a1 = one
    m2, l2, a2 = two
    top = jnp.maximum(m1, m2)
    w1, w2 = jnp.exp2(m1 - top), jnp.exp2(m2 - top)
    return top, l1 * w1 + l2 * w2, a1 * w1 + a2 * w2


def packed(m, l):
    lane = lax.broadcasted_iota(jnp.int32, (m.shape[0], 128), 1)
    return jnp.where(lane == 0, m, jnp.where(lane == 1, l, 0.0))


def kernel(
    seq_size, leaf_size, steps,
    q_hbm, prompt_hbm, node_hbm, len_hbm, anc_hbm, out_ref,
    q_in, q_rows, prompt, node, len_ref, anc_ref, qs, shared, lens, bias_ref,
    acc, stat, stat_t, got_acc, got_stat, pair_out, pair_in,
    load_sem, slot_send, slot_recv, len_send, len_recv,
    across_send, up_send, down_send, block_recv, acc_send, acc_recv, stat_send, stat_recv, pair_sem,
):
    pairs = seq_size // 2
    per_kv = pairs // KV_HEADS
    rows = q_rows.shape[0]
    pair_rows = (HEADS // pairs) * rows
    half_rows = pair_rows // 2
    slots, tokens = node.shape[1], node.shape[2]
    levels = anc_ref.shape[1]
    far = leaf_size // 2
    seq, leaf = lax.axis_index("seq"), lax.axis_index("leaf")
    pair, core = seq // 2, lax.rem(seq, 2)
    kv = pair // per_kv
    place = lax.rem(pair, per_kv)
    line, side = leaf // 2, lax.rem(leaf, 2)
    sibling = (pair * 2 + 1 - core, leaf)
    across = (seq, line * 2 + 1 - side)

    def pair_at(p):
        return (p * 2 + core, leaf)

    def leaf_at(n):
        return (seq, n)

    def kv_cols(k):
        return pl.ds(pl.multiple_of(k * HEAD_DIM, HEAD_DIM), HEAD_DIM)

    loads = [
        pltpu.make_async_copy(q_hbm, q_in, load_sem.at[0]),
        pltpu.make_async_copy(node_hbm, node, load_sem.at[1]),
        pltpu.make_async_copy(prompt_hbm, prompt, load_sem.at[2]),
    ]
    own_slot = pltpu.make_async_copy(
        node_hbm.at[:, slots - 1, :, kv_cols(kv)], shared.at[leaf, :, pair], load_sem.at[3]
    )
    small = [
        pltpu.make_async_copy(len_hbm, len_ref, load_sem.at[4]),
        pltpu.make_async_copy(anc_hbm, anc_ref, load_sem.at[5]),
    ]
    for load in [own_slot] + small + loads:
        load.start()

    barrier = pltpu.get_barrier_semaphore()
    for d in range(1, pairs):
        pl.semaphore_signal(barrier, inc=1, device_id=pair_at(lax.rem(pair + d, pairs)), device_id_type=MESH)
    for d in range(1, leaf_size):
        pl.semaphore_signal(barrier, inc=1, device_id=leaf_at(lax.rem(leaf + d, leaf_size)), device_id_type=MESH)
    pl.semaphore_signal(barrier, inc=1, device_id=sibling, device_id_type=MESH)
    for load in small:
        load.wait()
    lens[pl.ds(leaf, 1)] = jnp.full((1, 8, 128), len_ref[slots - 1], jnp.int32)
    pl.semaphore_wait(barrier, pairs + leaf_size - 1)

    slot_copies = []
    for d in range(1, pairs):
        to = lax.rem(pair + d, pairs)
        slot_copies.append(pltpu.make_async_remote_copy(
            src_ref=node_hbm.at[:, slots - 1, :, kv_cols(to // per_kv)],
            dst_ref=shared.at[leaf, :, pair],
            send_sem=slot_send.at[d], recv_sem=slot_recv.at[d],
            device_id=pair_at(to), device_id_type=MESH,
        ))
        slot_copies[-1].start()

    def piece_copy(source, e, target, sems):
        piece = shared.at[source, :, lax.rem(pair + e, pairs)]
        return pltpu.make_async_remote_copy(
            src_ref=piece, dst_ref=piece,
            send_sem=sems.at[source, e], recv_sem=block_recv.at[source, e],
            device_id=target, device_id_type=MESH,
        )

    up, down = leaf_at(leaf + 2), leaf_at(leaf - 2)
    can_up, can_down = line < far - 1, line > 0

    def send_own(e):
        @pl.when(can_up)
        def _():
            piece_copy(leaf, e, up, up_send).start()

        @pl.when(can_down)
        def _():
            piece_copy(leaf, e, down, down_send).start()

        piece_copy(leaf, e, across, across_send).start()

    def pass_on(t, e):
        @pl.when(line >= t)
        def _():
            source = leaf - 2 * t
            piece_copy(source, e, down, up_send).wait_recv()

            @pl.when(can_up)
            def _():
                piece_copy(source, e, up, up_send).start()

            piece_copy(source, e, across, across_send).start()

        @pl.when(line + t < far)
        def _():
            source = leaf + 2 * t
            piece_copy(source, e, up, down_send).wait_recv()

            @pl.when(can_down)
            def _():
                piece_copy(source, e, down, down_send).start()

            piece_copy(source, e, across, across_send).start()

    def wait_sent(e):
        for n in range(far):
            source = 2 * n + side
            piece_copy(source, e, across, across_send).wait_send()

            @pl.when((line >= n) & can_up)
            def _():
                piece_copy(source, e, up, up_send).wait_send()

            @pl.when((line <= n) & can_down)
            def _():
                piece_copy(source, e, down, down_send).wait_send()

    own_slot.wait()
    send_own(0)
    len_copies = []
    for d in range(1, leaf_size):
        len_copies.append(pltpu.make_async_remote_copy(
            src_ref=lens.at[leaf], dst_ref=lens.at[leaf],
            send_sem=len_send.at[d], recv_sem=len_recv.at[d],
            device_id=leaf_at(lax.rem(leaf + d, leaf_size)), device_id_type=MESH,
        ))
        len_copies[-1].start()

    loads[0].wait()
    for n in range(rows // steps):
        q_rows[n * steps:(n + 1) * steps, :] = q_in[n].astype(jnp.float32)
    for h in range(HEADS):
        qs[h // GROUP, (h % GROUP) * rows:(h % GROUP + 1) * rows, :] = (
            q_rows[:, h * HEAD_DIM:(h + 1) * HEAD_DIM].astype(jnp.bfloat16)
        )

    for d in range(1, pairs):
        slot_copies[pairs - 1 - d].wait_recv()
        send_own(d)

    anc = jnp.zeros((rows, levels), jnp.int32)
    row_leaf = lax.broadcasted_iota(jnp.int32, (rows, levels), 0) // steps
    for n in range(rows // steps):
        anc = jnp.where(row_leaf == n, anc_ref[n:n + 1, :], anc)
    width = slots * tokens
    col = lax.broadcasted_iota(jnp.int32, (1, width), 1)
    col_slot = col // tokens
    position = seq * tokens + col - col_slot * tokens
    held = jnp.zeros((1, width), jnp.int32)
    for n in range(slots):
        held = jnp.where(col_slot == n, len_ref[n], held)
    ident = leaf * slots + col_slot
    inside = position < held
    count = jnp.zeros((rows, width), jnp.float32)
    for level in range(levels - 1):
        count += jnp.where(anc[:, level:level + 1] == ident, 1.0, 0.0)
    step = lax.rem(lax.broadcasted_iota(jnp.int32, (rows, width), 0), steps)
    last = (anc[:, levels - 1:] == ident) & (position <= held - steps + step)
    count += jnp.where(last, 1.0, 0.0)
    bias_ref[...] = bias_of(jnp.where(inside, count, 0.0))

    loads[1].wait()
    loads[2].wait()

    def main(k, n):
        q = qs[k]
        cols = kv_cols(k)
        first = scores_of(q, prompt[0, :, cols])
        second = biased(scores_of(q, node[0, :, :, cols].reshape(width, HEAD_DIM)), bias_ref[...])
        m = jnp.maximum(jnp.max(first, axis=1, keepdims=True), jnp.max(second, axis=1, keepdims=True))
        first = jnp.exp2(first - m)
        second = jnp.exp2(second - m)
        l = jnp.sum(first, axis=1, keepdims=True) + jnp.sum(second, axis=1, keepdims=True)
        acc[n] = mix(first, prompt[1, :, cols]) + mix(second, node[1, :, :, cols].reshape(width, HEAD_DIM))
        both = packed(m, l)
        stat[n] = both
        stat_t[n] = both.T[:8]

    def send_part(n, place_there, to, slot):
        part = pl.ds(pl.multiple_of(place_there * pair_rows, pair_rows), pair_rows)
        copies = [
            pltpu.make_async_remote_copy(
                src_ref=acc.at[n, part], dst_ref=got_acc.at[slot],
                send_sem=acc_send.at[slot], recv_sem=acc_recv.at[slot],
                device_id=pair_at(to), device_id_type=MESH,
            ),
            pltpu.make_async_remote_copy(
                src_ref=stat_t.at[n], dst_ref=got_stat.at[slot],
                send_sem=stat_send.at[slot], recv_sem=stat_recv.at[slot],
                device_id=pair_at(to), device_id_type=MESH,
            ),
        ]
        for copy in copies:
            copy.start()
        return copies

    pass_on(1, 0)
    main(1 - kv, 0)
    parts = []
    for n in range(per_kv):
        place_there = lax.rem(place + n, per_kv)
        parts += send_part(0, place_there, (1 - kv) * per_kv + place_there, n)
    for e in range(1, pairs):
        pass_on(1, e)
    pass_on(2, 0)
    main(kv, 1)
    for e in range(1, pairs):
        pass_on(2, e)
    pass_on(3, 0)
    for n in range(1, per_kv):
        place_there = lax.rem(place + n, per_kv)
        parts += send_part(1, place_there, kv * per_kv + place_there, per_kv + n - 1)

    mine = pl.ds(pl.multiple_of(place * pair_rows, pair_rows), pair_rows)
    q_mine = qs[kv, mine]
    state = (stat[1, mine, 0:1], stat[1, mine, 1:2], acc[1, mine])

    for copy in len_copies:
        copy.wait_recv()
    span = pairs * tokens
    span_col = lax.broadcasted_iota(jnp.int32, (1, span), 1)
    span_block = span_col // tokens
    span_position = (span_block * 2 + core) * tokens + span_col - span_block * tokens

    def visit(state, source):
        m, l, total = state
        target = source * slots + slots - 1
        count = jnp.zeros((rows, 1), jnp.float32)
        for level in range(levels - 1):
            count += jnp.where(anc[:, level:level + 1] == target, 1.0, 0.0)
        bias = bias_of(jnp.where(span_position < lens[source][0:1, :span], count, 0.0))
        s = biased(scores_of(q_mine, shared[source, 0].reshape(span, HEAD_DIM)), bias)
        top = jnp.maximum(m, jnp.max(s, axis=1, keepdims=True))
        p = jnp.exp2(s - top)
        w = jnp.exp2(m - top)
        return (
            top,
            l * w + jnp.sum(p, axis=1, keepdims=True),
            total * w + mix(p, shared[source, 1].reshape(span, HEAD_DIM)),
        )

    def nearest(n):
        short = jnp.minimum(line, far - 1 - line)
        off = jnp.where(n < 2 * short, n // 2 + 1, n + 1 - short)
        below = jnp.where(n < 2 * short, n % 2 == 0, 2 * line > far - 1)
        return jnp.where(below, line - off, line + off) * 2

    def visit_across(state, source):
        for e in range(pairs):
            piece_copy(source, e, across, across_send).wait_recv()
        return visit(state, source)

    state = visit_across(state, line * 2 + 1 - side)
    state = visit(state, nearest(0) + side)
    for e in range(1, pairs):
        pass_on(3, e)
    for t in range(4, far):
        for e in range(pairs):
            pass_on(t, e)
    for n in range(1, far - 1):
        state = visit(state, nearest(n) + side)

    for n in range(pairs - 1):
        parts[2 * n].wait_recv()
        parts[2 * n + 1].wait_recv()
        stats = jnp.concatenate([got_stat[n], jnp.zeros((120, GROUP * rows), jnp.float32)], axis=0).T
        stat[0] = stats
        state = merge(state, (stat[0, mine, 0:1], stat[0, mine, 1:2], got_acc[n]))

    for n in range(far - 1):
        state = visit_across(state, nearest(n) + 1 - side)

    pair_out[:, HEAD_DIM:] = packed(state[0], state[1])
    pair_out[:, :HEAD_DIM] = state[2]

    def half(n):
        return pl.ds(pl.multiple_of(n * half_rows, half_rows), half_rows)

    swap = pltpu.make_async_remote_copy(
        src_ref=pair_out.at[half(1 - core)], dst_ref=pair_in,
        send_sem=pair_sem.at[0], recv_sem=pair_sem.at[1],
        device_id=sibling, device_id_type=MESH,
    )
    swap.start()
    kept = pair_out[half(core)]
    swap.wait_recv()
    came = pair_in[...]
    _, l, total = merge(
        (kept[:, HEAD_DIM:HEAD_DIM + 1], kept[:, HEAD_DIM + 1:HEAD_DIM + 2], kept[:, :HEAD_DIM]),
        (came[:, HEAD_DIM:HEAD_DIM + 1], came[:, HEAD_DIM + 1:HEAD_DIM + 2], came[:, :HEAD_DIM]),
    )
    result = (total / l).astype(out_ref.dtype)
    for h in range(half_rows // rows):
        out_ref[:, h * HEAD_DIM:(h + 1) * HEAD_DIM] = result[h * rows:(h + 1) * rows]

    for e in range(pairs):
        wait_sent(e)
    for copy in slot_copies + len_copies + parts + [swap]:
        copy.wait_send()


def shards(seq_size, leaf_size, queries, prompt_kv, node_kv, node_lengths, ancestors):
    leaves, steps, feats = queries.shape
    rows = leaves * steps
    slots, tokens, wide = node_kv.shape[1:]
    pairs = seq_size // 2
    pair_rows = (HEADS // pairs) * rows
    span = pairs * tokens
    kv_rows = GROUP * rows
    dma = pltpu.SemaphoreType.DMA
    out = pl.pallas_call(
        functools.partial(kernel, seq_size, leaf_size, steps),
        out_shape=jax.ShapeDtypeStruct((rows, feats // seq_size), jnp.bfloat16),
        in_specs=[pl.BlockSpec(memory_space=pl.ANY)] * 5,
        out_specs=pl.BlockSpec(memory_space=pltpu.VMEM),
        scratch_shapes=[
            pltpu.VMEM(queries.shape, jnp.bfloat16),
            pltpu.VMEM((rows, feats), jnp.float32),
            pltpu.VMEM(prompt_kv.shape, jnp.bfloat16),
            pltpu.VMEM(node_kv.shape, jnp.bfloat16),
            pltpu.SMEM(node_lengths.shape, jnp.int32),
            pltpu.VMEM(ancestors.shape, jnp.int32),
            pltpu.VMEM((KV_HEADS, kv_rows, HEAD_DIM), jnp.bfloat16),
            pltpu.VMEM((leaf_size, 2, pairs, tokens, HEAD_DIM), jnp.bfloat16),
            pltpu.VMEM((leaf_size, 8, 128), jnp.int32),
            pltpu.VMEM((rows, slots * tokens), jnp.float32),
            pltpu.VMEM((2, kv_rows, HEAD_DIM), jnp.float32),
            pltpu.VMEM((2, kv_rows, 128), jnp.float32),
            pltpu.VMEM((2, 8, kv_rows), jnp.float32),
            pltpu.VMEM((pairs - 1, pair_rows, HEAD_DIM), jnp.float32),
            pltpu.VMEM((pairs - 1, 8, kv_rows), jnp.float32),
            pltpu.VMEM((pair_rows, HEAD_DIM + 128), jnp.float32),
            pltpu.VMEM((pair_rows // 2, HEAD_DIM + 128), jnp.float32),
            dma((6,)),
            dma((pairs,)), dma((pairs,)),
            dma((leaf_size,)), dma((leaf_size,)),
            dma((leaf_size, pairs)), dma((leaf_size, pairs)),
            dma((leaf_size, pairs)), dma((leaf_size, pairs)),
            dma((pairs,)), dma((pairs,)),
            dma((pairs,)), dma((pairs,)),
            dma((2,)),
        ],
        compiler_params=pltpu.CompilerParams(
            collective_id=0, has_side_effects=True, vmem_limit_bytes=121 * 512 * 1024
        ),
    )(queries, prompt_kv, node_kv, node_lengths, ancestors)
    return out.reshape(leaves, steps, feats // seq_size)


def solution(mesh):
    placed = (
        P("leaf", None, None),
        P(None, "seq", None),
        P(None, "leaf", "seq", None),
        P("leaf"),
        P("leaf", None),
    )
    return jax.shard_map(
        functools.partial(shards, mesh.shape["seq"], mesh.shape["leaf"]),
        mesh=mesh, in_specs=placed, out_specs=P("leaf", None, "seq"), check_vma=False,
    )
```

```python
import functools
import math

import jax
import jax.numpy as jnp
from jax import lax
from jax.experimental import pallas as pl
from jax.experimental.pallas import tpu as pltpu
from jax.sharding import PartitionSpec as P

HEADS = 16
KV_HEADS = 2
HEAD_DIM = 256
GROUP = HEADS // KV_HEADS
HIDDEN = -1e30
LOG2E = 1.4426950408889634
MESH = pl.DeviceIdType.MESH


def scores_of(q, keys):
    dims = (((1,), (1,)), ((), ()))
    raw = lax.dot_general(q, keys, dims, preferred_element_type=jnp.float32)
    return raw * (LOG2E / math.sqrt(HEAD_DIM))


def biased(scores, bias):
    rows, cols = scores.shape
    per = bias.shape[0]
    return (scores.reshape(rows // per, per, cols) + bias[None]).reshape(rows, cols)


def bias_of(count):
    extra = jnp.where(count > 1.5, jnp.log(jnp.maximum(count, 1.0)) * LOG2E, 0.0)
    return jnp.where(count > 0.5, extra, HIDDEN)


def mix(p, values):
    return jnp.dot(p.astype(jnp.bfloat16), values, preferred_element_type=jnp.float32)


def merge(one, two):
    m1, l1, a1 = one
    m2, l2, a2 = two
    top = jnp.maximum(m1, m2)
    w1, w2 = jnp.exp2(m1 - top), jnp.exp2(m2 - top)
    return top, l1 * w1 + l2 * w2, a1 * w1 + a2 * w2


def packed(m, l):
    lane = lax.broadcasted_iota(jnp.int32, (m.shape[0], 128), 1)
    return jnp.where(lane == 0, m, jnp.where(lane == 1, l, 0.0))


def kernel(
    seq_size, leaf_size, steps,
    q_hbm, prompt_hbm, node_hbm, len_hbm, anc_hbm, out_ref,
    q_in, q_rows, prompt, node, len_ref, anc_ref, qs, shared, lens, bias_ref,
    acc, stat, stat_t, got_acc, got_stat, pair_out, pair_in,
    load_sem, slot_send, slot_recv, len_send, len_recv,
    across_send, up_send, down_send, block_recv, acc_send, acc_recv, stat_send, stat_recv, pair_sem,
):
    pairs = seq_size // 2
    per_kv = pairs // KV_HEADS
    rows = q_rows.shape[0]
    pair_rows = (HEADS // pairs) * rows
    half_rows = pair_rows // 2
    slots, tokens = node.shape[1], node.shape[2]
    levels = anc_ref.shape[1]
    far = leaf_size // 2
    seq, leaf = lax.axis_index("seq"), lax.axis_index("leaf")
    pair, core = seq // 2, lax.rem(seq, 2)
    kv = pair // per_kv
    place = lax.rem(pair, per_kv)
    line, side = leaf // 2, lax.rem(leaf, 2)
    sibling = (pair * 2 + 1 - core, leaf)
    across = (seq, line * 2 + 1 - side)

    def pair_at(p):
        return (p * 2 + core, leaf)

    def leaf_at(n):
        return (seq, n)

    def kv_cols(k):
        return pl.ds(pl.multiple_of(k * HEAD_DIM, HEAD_DIM), HEAD_DIM)

    loads = [
        pltpu.make_async_copy(q_hbm, q_in, load_sem.at[0]),
        pltpu.make_async_copy(node_hbm, node, load_sem.at[1]),
        pltpu.make_async_copy(prompt_hbm, prompt, load_sem.at[2]),
    ]
    own_slot = pltpu.make_async_copy(
        node_hbm.at[:, slots - 1, :, kv_cols(kv)], shared.at[leaf, :, pair], load_sem.at[3]
    )
    small = [
        pltpu.make_async_copy(len_hbm, len_ref, load_sem.at[4]),
        pltpu.make_async_copy(anc_hbm, anc_ref, load_sem.at[5]),
    ]
    for load in [own_slot] + small + loads:
        load.start()

    barrier = pltpu.get_barrier_semaphore()
    for d in range(1, pairs):
        pl.semaphore_signal(barrier, inc=1, device_id=pair_at(lax.rem(pair + d, pairs)), device_id_type=MESH)
    for d in range(1, leaf_size):
        pl.semaphore_signal(barrier, inc=1, device_id=leaf_at(lax.rem(leaf + d, leaf_size)), device_id_type=MESH)
    pl.semaphore_signal(barrier, inc=1, device_id=sibling, device_id_type=MESH)
    for load in small:
        load.wait()
    lens[pl.ds(leaf, 1)] = jnp.full((1, 8, 128), len_ref[slots - 1], jnp.int32)
    pl.semaphore_wait(barrier, pairs + leaf_size - 1)

    slot_copies = []
    for d in range(1, pairs):
        to = lax.rem(pair + d, pairs)
        slot_copies.append(pltpu.make_async_remote_copy(
            src_ref=node_hbm.at[:, slots - 1, :, kv_cols(to // per_kv)],
            dst_ref=shared.at[leaf, :, pair],
            send_sem=slot_send.at[d], recv_sem=slot_recv.at[d],
            device_id=pair_at(to), device_id_type=MESH,
        ))
        slot_copies[-1].start()

    def piece_copy(source, e, target, sems):
        piece = shared.at[source, :, lax.rem(pair + e, pairs)]
        return pltpu.make_async_remote_copy(
            src_ref=piece, dst_ref=piece,
            send_sem=sems.at[source, e], recv_sem=block_recv.at[source, e],
            device_id=target, device_id_type=MESH,
        )

    up, down = leaf_at(leaf + 2), leaf_at(leaf - 2)
    can_up, can_down = line < far - 1, line > 0

    def send_own(e):
        @pl.when(can_up)
        def _():
            piece_copy(leaf, e, up, up_send).start()

        @pl.when(can_down)
        def _():
            piece_copy(leaf, e, down, down_send).start()

        piece_copy(leaf, e, across, across_send).start()

    def pass_on(t, e):
        @pl.when(line >= t)
        def _():
            source = leaf - 2 * t
            piece_copy(source, e, down, up_send).wait_recv()

            @pl.when(can_up)
            def _():
                piece_copy(source, e, up, up_send).start()

            piece_copy(source, e, across, across_send).start()

        @pl.when(line + t < far)
        def _():
            source = leaf + 2 * t
            piece_copy(source, e, up, down_send).wait_recv()

            @pl.when(can_down)
            def _():
                piece_copy(source, e, down, down_send).start()

            piece_copy(source, e, across, across_send).start()

    def wait_sent(e):
        for n in range(far):
            source = 2 * n + side
            piece_copy(source, e, across, across_send).wait_send()

            @pl.when((line >= n) & can_up)
            def _():
                piece_copy(source, e, up, up_send).wait_send()

            @pl.when((line <= n) & can_down)
            def _():
                piece_copy(source, e, down, down_send).wait_send()

    own_slot.wait()
    send_own(0)
    len_copies = []
    for d in range(1, leaf_size):
        len_copies.append(pltpu.make_async_remote_copy(
            src_ref=lens.at[leaf], dst_ref=lens.at[leaf],
            send_sem=len_send.at[d], recv_sem=len_recv.at[d],
            device_id=leaf_at(lax.rem(leaf + d, leaf_size)), device_id_type=MESH,
        ))
        len_copies[-1].start()

    loads[0].wait()
    for n in range(rows // steps):
        q_rows[n * steps:(n + 1) * steps, :] = q_in[n].astype(jnp.float32)
    for h in range(HEADS):
        qs[h // GROUP, (h % GROUP) * rows:(h % GROUP + 1) * rows, :] = (
            q_rows[:, h * HEAD_DIM:(h + 1) * HEAD_DIM].astype(jnp.bfloat16)
        )

    for d in range(1, pairs):
        slot_copies[pairs - 1 - d].wait_recv()
        send_own(d)

    anc = jnp.zeros((rows, levels), jnp.int32)
    row_leaf = lax.broadcasted_iota(jnp.int32, (rows, levels), 0) // steps
    for n in range(rows // steps):
        anc = jnp.where(row_leaf == n, anc_ref[n:n + 1, :], anc)
    width = slots * tokens
    col = lax.broadcasted_iota(jnp.int32, (1, width), 1)
    col_slot = col // tokens
    position = seq * tokens + col - col_slot * tokens
    held = jnp.zeros((1, width), jnp.int32)
    for n in range(slots):
        held = jnp.where(col_slot == n, len_ref[n], held)
    ident = leaf * slots + col_slot
    inside = position < held
    count = jnp.zeros((rows, width), jnp.float32)
    for level in range(levels - 1):
        count += jnp.where(anc[:, level:level + 1] == ident, 1.0, 0.0)
    step = lax.rem(lax.broadcasted_iota(jnp.int32, (rows, width), 0), steps)
    last = (anc[:, levels - 1:] == ident) & (position <= held - steps + step)
    count += jnp.where(last, 1.0, 0.0)
    bias_ref[...] = bias_of(jnp.where(inside, count, 0.0))

    loads[1].wait()
    loads[2].wait()

    def weigh(k):
        q = qs[k]
        cols = kv_cols(k)
        first = scores_of(q, prompt[0, :, cols])
        second = biased(scores_of(q, node[0, :, :, cols].reshape(width, HEAD_DIM)), bias_ref[...])
        m = jnp.maximum(jnp.max(first, axis=1, keepdims=True), jnp.max(second, axis=1, keepdims=True))
        first = jnp.exp2(first - m)
        second = jnp.exp2(second - m)
        l = jnp.sum(first, axis=1, keepdims=True) + jnp.sum(second, axis=1, keepdims=True)
        return first.astype(jnp.bfloat16), second.astype(jnp.bfloat16), m, l

    def add_up(k, n, weighed):
        first, second, m, l = weighed
        cols = kv_cols(k)
        acc[n] = mix(first, prompt[1, :, cols]) + mix(second, node[1, :, :, cols].reshape(width, HEAD_DIM))
        both = packed(m, l)
        stat[n] = both
        stat_t[n] = both.T[:8]

    def send_part(n, place_there, to, slot):
        part = pl.ds(pl.multiple_of(place_there * pair_rows, pair_rows), pair_rows)
        copies = [
            pltpu.make_async_remote_copy(
                src_ref=acc.at[n, part], dst_ref=got_acc.at[slot],
                send_sem=acc_send.at[slot], recv_sem=acc_recv.at[slot],
                device_id=pair_at(to), device_id_type=MESH,
            ),
            pltpu.make_async_remote_copy(
                src_ref=stat_t.at[n], dst_ref=got_stat.at[slot],
                send_sem=stat_send.at[slot], recv_sem=stat_recv.at[slot],
                device_id=pair_at(to), device_id_type=MESH,
            ),
        ]
        for copy in copies:
            copy.start()
        return copies

    pass_on(1, 0)
    weighed = weigh(1 - kv)
    for e in range(1, pairs):
        pass_on(1, e)
    add_up(1 - kv, 0, weighed)
    parts = []
    for n in range(per_kv):
        place_there = lax.rem(place + n, per_kv)
        parts += send_part(0, place_there, (1 - kv) * per_kv + place_there, n)
    pass_on(2, 0)
    weighed = weigh(kv)
    for e in range(1, pairs):
        pass_on(2, e)
    add_up(kv, 1, weighed)
    for n in range(1, per_kv):
        place_there = lax.rem(place + n, per_kv)
        parts += send_part(1, place_there, kv * per_kv + place_there, per_kv + n - 1)
    pass_on(3, 0)

    mine = pl.ds(pl.multiple_of(place * pair_rows, pair_rows), pair_rows)
    q_mine = qs[kv, mine]
    state = (stat[1, mine, 0:1], stat[1, mine, 1:2], acc[1, mine])

    for copy in len_copies:
        copy.wait_recv()
    span = pairs * tokens
    span_col = lax.broadcasted_iota(jnp.int32, (1, span), 1)
    span_block = span_col // tokens
    span_position = (span_block * 2 + core) * tokens + span_col - span_block * tokens

    def visit(state, source):
        m, l, total = state
        target = source * slots + slots - 1
        count = jnp.zeros((rows, 1), jnp.float32)
        for level in range(levels - 1):
            count += jnp.where(anc[:, level:level + 1] == target, 1.0, 0.0)
        bias = bias_of(jnp.where(span_position < lens[source][0:1, :span], count, 0.0))
        s = biased(scores_of(q_mine, shared[source, 0].reshape(span, HEAD_DIM)), bias)
        top = jnp.maximum(m, jnp.max(s, axis=1, keepdims=True))
        p = jnp.exp2(s - top)
        w = jnp.exp2(m - top)
        return (
            top,
            l * w + jnp.sum(p, axis=1, keepdims=True),
            total * w + mix(p, shared[source, 1].reshape(span, HEAD_DIM)),
        )

    def nearest(n):
        short = jnp.minimum(line, far - 1 - line)
        off = jnp.where(n < 2 * short, n // 2 + 1, n + 1 - short)
        below = jnp.where(n < 2 * short, n % 2 == 0, 2 * line > far - 1)
        return jnp.where(below, line - off, line + off) * 2

    def visit_across(state, source):
        for e in range(pairs):
            piece_copy(source, e, across, across_send).wait_recv()
        return visit(state, source)

    state = visit_across(state, line * 2 + 1 - side)
    for e in range(1, pairs):
        pass_on(3, e)
    state = visit(state, nearest(0) + side)
    for t in range(4, far):
        for e in range(pairs):
            pass_on(t, e)
    for n in range(1, far - 1):
        state = visit(state, nearest(n) + side)

    for n in range(pairs - 1):
        parts[2 * n].wait_recv()
        parts[2 * n + 1].wait_recv()
        stats = jnp.concatenate([got_stat[n], jnp.zeros((120, GROUP * rows), jnp.float32)], axis=0).T
        stat[0] = stats
        state = merge(state, (stat[0, mine, 0:1], stat[0, mine, 1:2], got_acc[n]))

    for n in range(far - 1):
        state = visit_across(state, nearest(n) + 1 - side)

    pair_out[:, HEAD_DIM:] = packed(state[0], state[1])
    pair_out[:, :HEAD_DIM] = state[2]

    def half(n):
        return pl.ds(pl.multiple_of(n * half_rows, half_rows), half_rows)

    swap = pltpu.make_async_remote_copy(
        src_ref=pair_out.at[half(1 - core)], dst_ref=pair_in,
        send_sem=pair_sem.at[0], recv_sem=pair_sem.at[1],
        device_id=sibling, device_id_type=MESH,
    )
    swap.start()
    kept = pair_out[half(core)]
    swap.wait_recv()
    came = pair_in[...]
    _, l, total = merge(
        (kept[:, HEAD_DIM:HEAD_DIM + 1], kept[:, HEAD_DIM + 1:HEAD_DIM + 2], kept[:, :HEAD_DIM]),
        (came[:, HEAD_DIM:HEAD_DIM + 1], came[:, HEAD_DIM + 1:HEAD_DIM + 2], came[:, :HEAD_DIM]),
    )
    result = total / l
    for h in range(half_rows // rows):
        q_rows[:, h * HEAD_DIM:(h + 1) * HEAD_DIM] = result[h * rows:(h + 1) * rows]
    for n in range(rows // steps):
        out_ref[n] = q_rows[n * steps:(n + 1) * steps, :out_ref.shape[2]].astype(out_ref.dtype)

    for e in range(pairs):
        wait_sent(e)
    for copy in slot_copies + len_copies + parts + [swap]:
        copy.wait_send()


def shards(seq_size, leaf_size, queries, prompt_kv, node_kv, node_lengths, ancestors):
    leaves, steps, feats = queries.shape
    rows = leaves * steps
    slots, tokens, wide = node_kv.shape[1:]
    pairs = seq_size // 2
    pair_rows = (HEADS // pairs) * rows
    span = pairs * tokens
    kv_rows = GROUP * rows
    dma = pltpu.SemaphoreType.DMA
    return pl.pallas_call(
        functools.partial(kernel, seq_size, leaf_size, steps),
        out_shape=jax.ShapeDtypeStruct((leaves, steps, feats // seq_size), jnp.bfloat16),
        in_specs=[pl.BlockSpec(memory_space=pl.ANY)] * 5,
        out_specs=pl.BlockSpec(memory_space=pltpu.VMEM),
        scratch_shapes=[
            pltpu.VMEM(queries.shape, jnp.bfloat16),
            pltpu.VMEM((rows, feats), jnp.float32),
            pltpu.VMEM(prompt_kv.shape, jnp.bfloat16),
            pltpu.VMEM(node_kv.shape, jnp.bfloat16),
            pltpu.SMEM(node_lengths.shape, jnp.int32),
            pltpu.VMEM(ancestors.shape, jnp.int32),
            pltpu.VMEM((KV_HEADS, kv_rows, HEAD_DIM), jnp.bfloat16),
            pltpu.VMEM((leaf_size, 2, pairs, tokens, HEAD_DIM), jnp.bfloat16),
            pltpu.VMEM((leaf_size, 8, 128), jnp.int32),
            pltpu.VMEM((rows, slots * tokens), jnp.float32),
            pltpu.VMEM((2, kv_rows, HEAD_DIM), jnp.float32),
            pltpu.VMEM((2, kv_rows, 128), jnp.float32),
            pltpu.VMEM((2, 8, kv_rows), jnp.float32),
            pltpu.VMEM((pairs - 1, pair_rows, HEAD_DIM), jnp.float32),
            pltpu.VMEM((pairs - 1, 8, kv_rows), jnp.float32),
            pltpu.VMEM((pair_rows, HEAD_DIM + 128), jnp.float32),
            pltpu.VMEM((pair_rows // 2, HEAD_DIM + 128), jnp.float32),
            dma((6,)),
            dma((pairs,)), dma((pairs,)),
            dma((leaf_size,)), dma((leaf_size,)),
            dma((leaf_size, pairs)), dma((leaf_size, pairs)),
            dma((leaf_size, pairs)), dma((leaf_size, pairs)),
            dma((pairs,)), dma((pairs,)),
            dma((pairs,)), dma((pairs,)),
            dma((2,)),
        ],
        compiler_params=pltpu.CompilerParams(
            collective_id=0, has_side_effects=True, vmem_limit_bytes=121 * 512 * 1024
        ),
    )(queries, prompt_kv, node_kv, node_lengths, ancestors)


def solution(mesh):
    placed = (
        P("leaf", None, None),
        P(None, "seq", None),
        P(None, "leaf", "seq", None),
        P("leaf"),
        P("leaf", None),
    )
    return jax.shard_map(
        functools.partial(shards, mesh.shape["seq"], mesh.shape["leaf"]),
        mesh=mesh, in_specs=placed, out_specs=P("leaf", None, "seq"), check_vma=False,
    )
```

```python
import functools
import math

import jax
import jax.numpy as jnp
from jax import lax
from jax.experimental import pallas as pl
from jax.experimental.pallas import tpu as pltpu
from jax.sharding import PartitionSpec as P

HEADS = 16
KV_HEADS = 2
HEAD_DIM = 256
GROUP = HEADS // KV_HEADS
HIDDEN = -1e30
LOG2E = 1.4426950408889634
MESH = pl.DeviceIdType.MESH


def scores_of(q, keys):
    dims = (((1,), (1,)), ((), ()))
    raw = lax.dot_general(q, keys, dims, preferred_element_type=jnp.float32)
    return raw * (LOG2E / math.sqrt(HEAD_DIM))


def biased(scores, bias):
    rows, cols = scores.shape
    per = bias.shape[0]
    return (scores.reshape(rows // per, per, cols) + bias[None]).reshape(rows, cols)


def bias_of(count):
    extra = jnp.where(count > 1.5, jnp.log(jnp.maximum(count, 1.0)) * LOG2E, 0.0)
    return jnp.where(count > 0.5, extra, HIDDEN)


def mix(p, values):
    return jnp.dot(p.astype(jnp.bfloat16), values, preferred_element_type=jnp.float32)


def merge(one, two):
    m1, l1, a1 = one
    m2, l2, a2 = two
    top = jnp.maximum(m1, m2)
    w1, w2 = jnp.exp2(m1 - top), jnp.exp2(m2 - top)
    return top, l1 * w1 + l2 * w2, a1 * w1 + a2 * w2


def packed(m, l):
    lane = lax.broadcasted_iota(jnp.int32, (m.shape[0], 128), 1)
    return jnp.where(lane == 0, m, jnp.where(lane == 1, l, 0.0))


def kernel(
    seq_size, leaf_size, steps,
    q_hbm, prompt_hbm, node_hbm, len_hbm, anc_hbm, out_ref,
    q_in, q_rows, prompt, node, len_ref, anc_ref, qs, shared, lens, bias_ref,
    acc, stat, stat_t, got_acc, got_stat, pair_out, pair_in,
    load_sem, slot_send, slot_recv, len_send, len_recv,
    across_send, up_send, down_send, block_recv, acc_send, acc_recv, stat_send, stat_recv, pair_sem,
):
    pairs = seq_size // 2
    per_kv = pairs // KV_HEADS
    rows = q_rows.shape[0]
    pair_rows = (HEADS // pairs) * rows
    half_rows = pair_rows // 2
    slots, tokens = node.shape[1], node.shape[2]
    levels = anc_ref.shape[1]
    far = leaf_size // 2
    seq, leaf = lax.axis_index("seq"), lax.axis_index("leaf")
    pair, core = seq // 2, lax.rem(seq, 2)
    kv = pair // per_kv
    place = lax.rem(pair, per_kv)
    line, side = leaf // 2, lax.rem(leaf, 2)
    sibling = (pair * 2 + 1 - core, leaf)
    across = (seq, line * 2 + 1 - side)

    def pair_at(p):
        return (p * 2 + core, leaf)

    def leaf_at(n):
        return (seq, n)

    def kv_cols(k):
        return pl.ds(pl.multiple_of(k * HEAD_DIM, HEAD_DIM), HEAD_DIM)

    loads = [
        pltpu.make_async_copy(q_hbm, q_in, load_sem.at[0]),
        pltpu.make_async_copy(node_hbm, node, load_sem.at[1]),
        pltpu.make_async_copy(prompt_hbm, prompt, load_sem.at[2]),
    ]
    own_slot = pltpu.make_async_copy(
        node_hbm.at[:, slots - 1, :, kv_cols(kv)], shared.at[leaf, :, pair], load_sem.at[3]
    )
    small = [
        pltpu.make_async_copy(len_hbm, len_ref, load_sem.at[4]),
        pltpu.make_async_copy(anc_hbm, anc_ref, load_sem.at[5]),
    ]
    for load in [own_slot] + small + loads:
        load.start()

    barrier = pltpu.get_barrier_semaphore()
    for d in range(1, pairs):
        pl.semaphore_signal(barrier, inc=1, device_id=pair_at(lax.rem(pair + d, pairs)), device_id_type=MESH)
    for d in range(1, leaf_size):
        pl.semaphore_signal(barrier, inc=1, device_id=leaf_at(lax.rem(leaf + d, leaf_size)), device_id_type=MESH)
    pl.semaphore_signal(barrier, inc=1, device_id=sibling, device_id_type=MESH)
    for load in small:
        load.wait()
    lens[pl.ds(leaf, 1)] = jnp.full((1, 8, 128), len_ref[slots - 1], jnp.int32)
    pl.semaphore_wait(barrier, pairs + leaf_size - 1)

    slot_copies = []
    for d in range(1, pairs):
        to = lax.rem(pair + d, pairs)
        slot_copies.append(pltpu.make_async_remote_copy(
            src_ref=node_hbm.at[:, slots - 1, :, kv_cols(to // per_kv)],
            dst_ref=shared.at[leaf, :, pair],
            send_sem=slot_send.at[d], recv_sem=slot_recv.at[d],
            device_id=pair_at(to), device_id_type=MESH,
        ))
        slot_copies[-1].start()

    def piece_copy(source, e, target, sems):
        piece = shared.at[source, :, lax.rem(pair + e, pairs)]
        return pltpu.make_async_remote_copy(
            src_ref=piece, dst_ref=piece,
            send_sem=sems.at[source, e], recv_sem=block_recv.at[source, e],
            device_id=target, device_id_type=MESH,
        )

    up, down = leaf_at(leaf + 2), leaf_at(leaf - 2)
    can_up, can_down = line < far - 1, line > 0

    def send_own(e):
        @pl.when(can_up)
        def _():
            piece_copy(leaf, e, up, up_send).start()

        @pl.when(can_down)
        def _():
            piece_copy(leaf, e, down, down_send).start()

        piece_copy(leaf, e, across, across_send).start()

    def pass_on(t, e):
        @pl.when(line >= t)
        def _():
            source = leaf - 2 * t
            piece_copy(source, e, down, up_send).wait_recv()

            @pl.when(can_up)
            def _():
                piece_copy(source, e, up, up_send).start()

            piece_copy(source, e, across, across_send).start()

        @pl.when(line + t < far)
        def _():
            source = leaf + 2 * t
            piece_copy(source, e, up, down_send).wait_recv()

            @pl.when(can_down)
            def _():
                piece_copy(source, e, down, down_send).start()

            piece_copy(source, e, across, across_send).start()

    def wait_sent(e):
        for n in range(far):
            source = 2 * n + side
            piece_copy(source, e, across, across_send).wait_send()

            @pl.when((line >= n) & can_up)
            def _():
                piece_copy(source, e, up, up_send).wait_send()

            @pl.when((line <= n) & can_down)
            def _():
                piece_copy(source, e, down, down_send).wait_send()

    own_slot.wait()
    send_own(0)
    len_copies = []
    for d in range(1, leaf_size):
        len_copies.append(pltpu.make_async_remote_copy(
            src_ref=lens.at[leaf], dst_ref=lens.at[leaf],
            send_sem=len_send.at[d], recv_sem=len_recv.at[d],
            device_id=leaf_at(lax.rem(leaf + d, leaf_size)), device_id_type=MESH,
        ))
        len_copies[-1].start()

    loads[0].wait()
    for n in range(rows // steps):
        q_rows[n * steps:(n + 1) * steps, :] = q_in[n].astype(jnp.float32)
    for h in range(HEADS):
        qs[h // GROUP, (h % GROUP) * rows:(h % GROUP + 1) * rows, :] = (
            q_rows[:, h * HEAD_DIM:(h + 1) * HEAD_DIM].astype(jnp.bfloat16)
        )

    for d in range(1, pairs):
        slot_copies[pairs - 1 - d].wait_recv()
        send_own(d)

    anc = jnp.zeros((rows, levels), jnp.int32)
    row_leaf = lax.broadcasted_iota(jnp.int32, (rows, levels), 0) // steps
    for n in range(rows // steps):
        anc = jnp.where(row_leaf == n, anc_ref[n:n + 1, :], anc)
    width = slots * tokens
    col = lax.broadcasted_iota(jnp.int32, (1, width), 1)
    col_slot = col // tokens
    position = seq * tokens + col - col_slot * tokens
    held = jnp.zeros((1, width), jnp.int32)
    for n in range(slots):
        held = jnp.where(col_slot == n, len_ref[n], held)
    ident = leaf * slots + col_slot
    inside = position < held
    count = jnp.zeros((rows, width), jnp.float32)
    for level in range(levels - 1):
        count += jnp.where(anc[:, level:level + 1] == ident, 1.0, 0.0)
    step = lax.rem(lax.broadcasted_iota(jnp.int32, (rows, width), 0), steps)
    last = (anc[:, levels - 1:] == ident) & (position <= held - steps + step)
    count += jnp.where(last, 1.0, 0.0)
    bias_ref[...] = bias_of(jnp.where(inside, count, 0.0))

    loads[1].wait()
    loads[2].wait()

    def weigh(k):
        q = qs[k]
        cols = kv_cols(k)
        first = scores_of(q, prompt[0, :, cols])
        second = biased(scores_of(q, node[0, :, :, cols].reshape(width, HEAD_DIM)), bias_ref[...])
        m = jnp.maximum(jnp.max(first, axis=1, keepdims=True), jnp.max(second, axis=1, keepdims=True))
        first = jnp.exp2(first - m)
        second = jnp.exp2(second - m)
        l = jnp.sum(first, axis=1, keepdims=True) + jnp.sum(second, axis=1, keepdims=True)
        return first.astype(jnp.bfloat16), second.astype(jnp.bfloat16), m, l

    def add_up(k, n, weighed):
        first, second, m, l = weighed
        cols = kv_cols(k)
        acc[n] = mix(first, prompt[1, :, cols]) + mix(second, node[1, :, :, cols].reshape(width, HEAD_DIM))
        both = packed(m, l)
        stat[n] = both
        stat_t[n] = both.T[:8]

    def send_part(n, place_there, to, slot):
        part = pl.ds(pl.multiple_of(place_there * pair_rows, pair_rows), pair_rows)
        copies = [
            pltpu.make_async_remote_copy(
                src_ref=acc.at[n, part], dst_ref=got_acc.at[slot],
                send_sem=acc_send.at[slot], recv_sem=acc_recv.at[slot],
                device_id=pair_at(to), device_id_type=MESH,
            ),
            pltpu.make_async_remote_copy(
                src_ref=stat_t.at[n], dst_ref=got_stat.at[slot],
                send_sem=stat_send.at[slot], recv_sem=stat_recv.at[slot],
                device_id=pair_at(to), device_id_type=MESH,
            ),
        ]
        for copy in copies:
            copy.start()
        return copies

    weighed = weigh(1 - kv)
    for e in range(pairs):
        pass_on(1, e)
    add_up(1 - kv, 0, weighed)
    parts = []
    for n in range(per_kv):
        place_there = lax.rem(place + n, per_kv)
        parts += send_part(0, place_there, (1 - kv) * per_kv + place_there, n)
    pass_on(2, 0)
    weighed = weigh(kv)
    for e in range(1, pairs):
        pass_on(2, e)
    add_up(kv, 1, weighed)
    for n in range(1, per_kv):
        place_there = lax.rem(place + n, per_kv)
        parts += send_part(1, place_there, kv * per_kv + place_there, per_kv + n - 1)
    pass_on(3, 0)

    mine = pl.ds(pl.multiple_of(place * pair_rows, pair_rows), pair_rows)
    q_mine = qs[kv, mine]
    state = (stat[1, mine, 0:1], stat[1, mine, 1:2], acc[1, mine])

    for copy in len_copies:
        copy.wait_recv()
    span = pairs * tokens
    span_col = lax.broadcasted_iota(jnp.int32, (1, span), 1)
    span_block = span_col // tokens
    span_position = (span_block * 2 + core) * tokens + span_col - span_block * tokens

    def visit(state, source):
        m, l, total = state
        target = source * slots + slots - 1
        count = jnp.zeros((rows, 1), jnp.float32)
        for level in range(levels - 1):
            count += jnp.where(anc[:, level:level + 1] == target, 1.0, 0.0)
        bias = bias_of(jnp.where(span_position < lens[source][0:1, :span], count, 0.0))
        s = biased(scores_of(q_mine, shared[source, 0].reshape(span, HEAD_DIM)), bias)
        top = jnp.maximum(m, jnp.max(s, axis=1, keepdims=True))
        p = jnp.exp2(s - top)
        w = jnp.exp2(m - top)
        return (
            top,
            l * w + jnp.sum(p, axis=1, keepdims=True),
            total * w + mix(p, shared[source, 1].reshape(span, HEAD_DIM)),
        )

    def nearest(n):
        short = jnp.minimum(line, far - 1 - line)
        off = jnp.where(n < 2 * short, n // 2 + 1, n + 1 - short)
        below = jnp.where(n < 2 * short, n % 2 == 0, 2 * line > far - 1)
        return jnp.where(below, line - off, line + off) * 2

    def visit_across(state, source):
        for e in range(pairs):
            piece_copy(source, e, across, across_send).wait_recv()
        return visit(state, source)

    state = visit_across(state, line * 2 + 1 - side)
    for e in range(1, pairs):
        pass_on(3, e)
    state = visit(state, nearest(0) + side)
    for t in range(4, far):
        for e in range(pairs):
            pass_on(t, e)
    for n in range(1, far - 1):
        state = visit(state, nearest(n) + side)

    for n in range(pairs - 1):
        parts[2 * n].wait_recv()
        parts[2 * n + 1].wait_recv()
        stats = jnp.concatenate([got_stat[n], jnp.zeros((120, GROUP * rows), jnp.float32)], axis=0).T
        stat[0] = stats
        state = merge(state, (stat[0, mine, 0:1], stat[0, mine, 1:2], got_acc[n]))

    for n in range(far - 1):
        state = visit_across(state, nearest(n) + 1 - side)

    pair_out[:, HEAD_DIM:] = packed(state[0], state[1])
    pair_out[:, :HEAD_DIM] = state[2]

    def half(n):
        return pl.ds(pl.multiple_of(n * half_rows, half_rows), half_rows)

    swap = pltpu.make_async_remote_copy(
        src_ref=pair_out.at[half(1 - core)], dst_ref=pair_in,
        send_sem=pair_sem.at[0], recv_sem=pair_sem.at[1],
        device_id=sibling, device_id_type=MESH,
    )
    swap.start()
    kept = pair_out[half(core)]
    swap.wait_recv()
    came = pair_in[...]
    _, l, total = merge(
        (kept[:, HEAD_DIM:HEAD_DIM + 1], kept[:, HEAD_DIM + 1:HEAD_DIM + 2], kept[:, :HEAD_DIM]),
        (came[:, HEAD_DIM:HEAD_DIM + 1], came[:, HEAD_DIM + 1:HEAD_DIM + 2], came[:, :HEAD_DIM]),
    )
    result = total / l
    for h in range(half_rows // rows):
        q_rows[:, h * HEAD_DIM:(h + 1) * HEAD_DIM] = result[h * rows:(h + 1) * rows]
    for n in range(rows // steps):
        out_ref[n] = q_rows[n * steps:(n + 1) * steps, :out_ref.shape[2]].astype(out_ref.dtype)

    for e in range(pairs):
        wait_sent(e)
    for copy in slot_copies + len_copies + parts + [swap]:
        copy.wait_send()


def shards(seq_size, leaf_size, queries, prompt_kv, node_kv, node_lengths, ancestors):
    leaves, steps, feats = queries.shape
    rows = leaves * steps
    slots, tokens, wide = node_kv.shape[1:]
    pairs = seq_size // 2
    pair_rows = (HEADS // pairs) * rows
    span = pairs * tokens
    kv_rows = GROUP * rows
    dma = pltpu.SemaphoreType.DMA
    return pl.pallas_call(
        functools.partial(kernel, seq_size, leaf_size, steps),
        out_shape=jax.ShapeDtypeStruct((leaves, steps, feats // seq_size), jnp.bfloat16),
        in_specs=[pl.BlockSpec(memory_space=pl.ANY)] * 5,
        out_specs=pl.BlockSpec(memory_space=pltpu.VMEM),
        scratch_shapes=[
            pltpu.VMEM(queries.shape, jnp.bfloat16),
            pltpu.VMEM((rows, feats), jnp.float32),
            pltpu.VMEM(prompt_kv.shape, jnp.bfloat16),
            pltpu.VMEM(node_kv.shape, jnp.bfloat16),
            pltpu.SMEM(node_lengths.shape, jnp.int32),
            pltpu.VMEM(ancestors.shape, jnp.int32),
            pltpu.VMEM((KV_HEADS, kv_rows, HEAD_DIM), jnp.bfloat16),
            pltpu.VMEM((leaf_size, 2, pairs, tokens, HEAD_DIM), jnp.bfloat16),
            pltpu.VMEM((leaf_size, 8, 128), jnp.int32),
            pltpu.VMEM((rows, slots * tokens), jnp.float32),
            pltpu.VMEM((2, kv_rows, HEAD_DIM), jnp.float32),
            pltpu.VMEM((2, kv_rows, 128), jnp.float32),
            pltpu.VMEM((2, 8, kv_rows), jnp.float32),
            pltpu.VMEM((pairs - 1, pair_rows, HEAD_DIM), jnp.float32),
            pltpu.VMEM((pairs - 1, 8, kv_rows), jnp.float32),
            pltpu.VMEM((pair_rows, HEAD_DIM + 128), jnp.float32),
            pltpu.VMEM((pair_rows // 2, HEAD_DIM + 128), jnp.float32),
            dma((6,)),
            dma((pairs,)), dma((pairs,)),
            dma((leaf_size,)), dma((leaf_size,)),
            dma((leaf_size, pairs)), dma((leaf_size, pairs)),
            dma((leaf_size, pairs)), dma((leaf_size, pairs)),
            dma((pairs,)), dma((pairs,)),
            dma((pairs,)), dma((pairs,)),
            dma((2,)),
        ],
        compiler_params=pltpu.CompilerParams(
            collective_id=0, has_side_effects=True, vmem_limit_bytes=121 * 512 * 1024
        ),
    )(queries, prompt_kv, node_kv, node_lengths, ancestors)


def solution(mesh):
    placed = (
        P("leaf", None, None),
        P(None, "seq", None),
        P(None, "leaf", "seq", None),
        P("leaf"),
        P("leaf", None),
    )
    return jax.shard_map(
        functools.partial(shards, mesh.shape["seq"], mesh.shape["leaf"]),
        mesh=mesh, in_specs=placed, out_specs=P("leaf", None, "seq"), check_vma=False,
    )
```
